32 devices in a mesh: dom: 16 (over z, x, core), rep: 2 (over y).
Axes of the slice: x: 2, y: 2, z: 4, core: 2. Of those that a mesh axis runs over, the one named last changes fastest.
Arguments:
- date_key: int32 [4096, 128], P('dom'), may hold values from 0 to 1791
- item_key: int32 [4096, 128], P('dom'), may hold values from 0 to 229375
- store_key: int32 [4096, 128], P('dom'), may hold values from 0 to 127
- measures: float32 [4096, 4, 128], P('dom'), may hold values from 0 to 2
- block_count: int32 [16], P('dom'), may hold values from 1 to 256, 1664 in all
- item_price: float32 [229376], P(('dom', 'rep')), may hold values from 0 to 1
- store_region: int32 [128], replicated, may hold values from 0 to 31
- date_flag: int32 [1792], replicated, may hold values 0 or 1
Outputs:
- region_profit: float32 [3, 32, 256], P(None, None, 'rep')
The draws below stay inside these ranges and needn't reach their ends.
Inputs may be any that keep to these rules, and one draw needn't show every extreme that they name: `block_count`: the live blocks of an index of dom are the first of its slots; the counts sum to 1664 and one index holds 256.
All inputs are finite; a program needn't handle non-finite values.
Results may differ from the reference program's by a relative error of at most 0.0028.
Values may be sent and summed in bfloat16 or wider, within the bound.
A program may use at most 64 MiB of HBM per device.

```python
import math
import jax
import jax.numpy as jnp
import numpy as np
from jax import lax

BLK = 128
SLOTS = 256
AGGS = 3
DATES = 1792
ITEMS = 229376
WEEKS = 256
STORES = 128
REGIONS = 32
BLOCKS = 4096
LIVE_TOTAL = 1664
N_DOM = 16


def plant(array, key, smallest, top_value):
    extent = array.shape
    spot = [jax.random.randint(jax.random.fold_in(key, axis), (), 0, extent[axis]) for axis in range(len(extent))]
    array = array.at[tuple(spot)].set(smallest)
    longest = extent.index(max(extent))
    spot[longest] = (spot[longest] + 1) % extent[longest]
    return array.at[tuple(spot)].set(top_value)


def shard_levels(stream_key, shape, shards, smallest, high):
    gain = 1.0
    for axis_at, shards_of in shards:
        heights = jax.random.uniform(jax.random.fold_in(jax.random.fold_in(stream_key, 6), axis_at), (shards_of,), jnp.float32, smallest / len(shards), high / len(shards))
        gain = gain * jnp.repeat(jnp.exp(heights), shape[axis_at] // shards_of).reshape((-1,) + (1,) * (len(shape) - 1 - axis_at))
    return gain


def rank_table(amount, skew):
    portions = [(1 << 20) // math.isqrt(rank ** skew) + 1 for rank in range(1, amount + 1)]
    width = 1 + sum(portions) // (1 << 30)
    return np.cumsum(np.array([max(1, weight // width) for weight in portions]))


def skewed_ids(rng, dims, count, slope):
    table = rank_table(count, slope)
    lot = jax.random.randint(jax.random.fold_in(rng, 1), dims, 0, int(table[count - 1]))
    rank = jnp.searchsorted(jnp.asarray(table, jnp.int32), lot, side="right")
    return jax.random.permutation(jax.random.fold_in(rng, 2), count)[rank].astype(jnp.int32)


def split_up(amount, total, limit, slope):
    portions = [(1 << 20) // math.isqrt(rank ** slope) + 1 for rank in range(2, amount + 1)]
    spare, given = total - limit - (amount - 1), [1] * (amount - 1)
    while spare > 0:
        candidates = [i for i in range(amount - 1) if given[i] < limit]
        mass, budget = sum([portions[i] for i in candidates]), spare
        for i in candidates:
            addition = min(limit - given[i], max(1, budget * portions[i] // mass), spare)
            given[i] = given[i] + addition
            spare = spare - addition
    return np.array([limit] + given)


def ragged_sizes(own_key, count, total, most, skew):
    if count == 2:
        one = jax.random.randint(own_key, (), max(1, total - most), min(most, total - 1) + 1)
        return jnp.stack([one, total - one])
    lengths = jnp.asarray(split_up(count, total, most, skew), jnp.int32)
    pairs = (count - 1) // 2
    donor, sink = lengths[1:1 + 2 * pairs:2], lengths[2:2 + 2 * pairs:2]
    room = jnp.minimum(donor - 1, most - sink)
    passed = jax.random.randint(jax.random.fold_in(own_key, 1), (pairs,), 0, 1 << 20) % (room + 1)
    lengths = lengths.at[1:1 + 2 * pairs:2].set(donor - passed).at[2:2 + 2 * pairs:2].set(sink + passed)
    return lengths[jax.random.permutation(jax.random.fold_in(own_key, 2), count)]


def setup_inputs(seed: int = 0) -> dict:
    keys = jax.random.split(jax.random.key(seed), 9)
    date_key = plant(jax.random.randint(keys[0], (BLOCKS, BLK), 0, DATES), jax.random.fold_in(keys[0], 1), 0, DATES - 1).astype(jnp.int32)
    item_key = plant(jax.random.randint(keys[1], (BLOCKS, BLK), 0, ITEMS), jax.random.fold_in(keys[1], 1), 0, ITEMS - 1).astype(jnp.int32)
    store_key = plant(skewed_ids(keys[2], (BLOCKS, BLK), STORES, 2), jax.random.fold_in(keys[2], 3), 0, STORES - 1).astype(jnp.int32)
    measures = jnp.clip(2.0 * jax.random.uniform(keys[3], (BLOCKS, 4, BLK), jnp.float32) ** shard_levels(keys[3], (BLOCKS, 4, BLK), ((0, 16),), -0.2, 0.2), 0.0, 2.0)
    block_count = ragged_sizes(keys[4], N_DOM, LIVE_TOTAL, SLOTS, 2).astype(jnp.int32)
    item_price = jnp.clip(1.0 * jax.random.uniform(keys[5], (ITEMS,), jnp.float32) ** shard_levels(keys[5], (ITEMS,), ((0, 32),), -0.2, 0.2), 0.0, 1.0)
    store_region = plant(jax.random.randint(keys[6], (STORES,), 0, REGIONS), jax.random.fold_in(keys[6], 1), 0, REGIONS - 1).astype(jnp.int32)
    date_flag = plant((jax.random.randint(keys[7], (DATES,), 0, 4) < 3).astype(jnp.int32), jax.random.fold_in(keys[7], 1), 0, 1)
    return dict(date_key=date_key, item_key=item_key, store_key=store_key, measures=measures, block_count=block_count, item_price=item_price, store_region=store_region, date_flag=date_flag)


low_price = 0.2
high_price = 0.8
week_length = 7


def reference(date_key, item_key, store_key, measures, block_count, item_price, store_region, date_flag):
    block_ids = jnp.arange(N_DOM * SLOTS, dtype=jnp.int32)
    holder = (block_ids // SLOTS).astype(jnp.int32)
    position = (block_ids % SLOTS).astype(jnp.int32)
    resident = position < jnp.take(block_count, holder)
    price_row = jnp.take(item_price, item_key)
    item_ok = (price_row >= low_price) & (price_row <= high_price)
    day_ok = jnp.take(date_flag, date_key) == 1
    passing = (resident[:, None] & item_ok & day_ok).astype(jnp.float32)
    quantity = measures[:, 0].astype(jnp.float32)
    selling = measures[:, 1].astype(jnp.float32)
    wholesale = measures[:, 2].astype(jnp.float32)
    coupon = measures[:, 3].astype(jnp.float32)
    profit = quantity * (selling - wholesale) - coupon
    revenue = quantity * selling - coupon
    stacked = jnp.stack([profit, revenue, quantity], axis=0) * passing[None]
    rounded = lax.optimization_barrier(stacked.astype(jnp.bfloat16)).astype(jnp.float32)
    group_key = (jnp.take(store_region, store_key) * WEEKS + date_key // week_length).astype(jnp.int32).reshape(-1)
    totals = [jax.ops.segment_sum(rounded[member].reshape(-1), group_key, num_segments=REGIONS * WEEKS) for member in range(AGGS)]
    return jnp.stack(totals).reshape(AGGS, REGIONS, WEEKS)
```

```python
import functools

import jax
import jax.numpy as jnp
import numpy as np
from jax import lax
from jax.experimental import pallas as pl
from jax.experimental.pallas import tpu as pltpu
from jax.sharding import PartitionSpec as P

MESH = pl.DeviceIdType.MESH
AGGS = 3
REG_DEV = 2
LANES = 128
low_price = 0.2
high_price = 0.8
week_length = 7


def round_up(value, step):
    return (value + step - 1) // step * step


def divider(divisor, limit):
    n = np.arange(limit, dtype=np.int64)
    for shift in range(8, 24):
        multiplier = -(-(1 << shift) // divisor)
        if (limit * multiplier) < (1 << 31) and np.array_equal((n * multiplier) >> shift, n // divisor):
            return multiplier, shift
    raise ValueError("no divider")


def lookup(row, lane):
    return jnp.take_along_axis(jnp.broadcast_to(row, lane.shape), lane, axis=1)


def kernel(
    dom_size, rep_size, regions, item_rows, slots, chunk,
    count_ref, date_hbm, item_hbm, store_hbm, meas_hbm, price_ref, region_ref, flag_ref,
    out_ref,
    date_v, item_v, store_v, meas_v, flags, words, reg_f, week_f, prof_f, rev_f, qty_f, lane_i, row_i, bit_i,
    acc, part, rbuf, fbuf,
    in_sem, z_send, z_recv, p_send, p_recv, q_send, q_recv, d_send, d_recv, c_send, c_recv,
    r_send, r_recv, f_send, f_recv,
):
    dom = lax.axis_index("dom")
    rep = lax.axis_index("rep")
    devices = dom_size * rep_size
    me = dom * rep_size + rep
    half = slots // rep_size
    outer_size = dom_size // 4
    outer = dom // 4
    mid = (dom // 2) % 2
    core = dom % 2

    base = pl.multiple_of(rep * half, 8)
    loads = [
        pltpu.make_async_copy(date_hbm.at[pl.ds(base, half)], date_v, in_sem.at[0]),
        pltpu.make_async_copy(item_hbm.at[pl.ds(base, half)], item_v, in_sem.at[1]),
        pltpu.make_async_copy(store_hbm.at[pl.ds(base, half)], store_v, in_sem.at[2]),
        pltpu.make_async_copy(meas_hbm.at[pl.ds(base * 4, half * 4)], meas_v, in_sem.at[3]),
    ]
    for load in loads:
        load.start()

    barrier = pltpu.get_barrier_semaphore()
    for k in range(1, devices):
        other = (me + k) % devices
        pl.semaphore_signal(
            barrier, inc=1, device_id={"dom": other // rep_size, "rep": other % rep_size}, device_id_type=MESH
        )

    padded = flags.shape[1]
    price = price_ref[...]
    power = jnp.left_shift(jnp.ones(price.shape, jnp.int32), me % 16).astype(jnp.float32)
    mark = jnp.where((price >= low_price) & (price <= high_price), power, 0.0)
    if padded > item_rows:
        mark = jnp.concatenate([mark, jnp.zeros((padded - item_rows, LANES), jnp.float32)], axis=0)
    flags[me] = mark.astype(jnp.bfloat16)
    pl.semaphore_wait(barrier, devices - 1)

    def index_of(o, m, c, r):
        return ((o * 2 + m) * 2 + c) * rep_size + r

    sends = []

    def send(block, to_dom, to_rep, s_sem, r_sem):
        copy = pltpu.make_async_remote_copy(
            src_ref=flags.at[block], dst_ref=flags.at[block], send_sem=s_sem, recv_sem=r_sem,
            device_id={"dom": to_dom, "rep": to_rep}, device_id_type=MESH,
        )
        copy.start()
        sends.append(copy)
        return copy

    dom_mid = dom + 2 - 4 * mid
    rep_other = (rep + 1) % rep_size
    dom_core = dom + 1 - 2 * core
    first_dom, first_rep = dom + (1 - core) * (2 - 4 * mid), rep + core * (rep_other - rep)
    second_dom, second_rep = dom + core * (2 - 4 * mid), rep + (1 - core) * (rep_other - rep)
    first_mid = mid + (1 - core) * (1 - 2 * mid)

    zc, pc, qc, dc, cc = {}, {}, {}, {}, {}

    def column(k):
        o = (outer + outer_size - k) % outer_size
        block = index_of(o, mid, core, rep)
        pc[k] = send(block, first_dom, first_rep, p_send.at[k], p_recv.at[k])
        qc[k] = send(block, second_dom, second_rep, q_send.at[k], q_recv.at[k])
        cc[0, k] = send(block, dom_core, rep, c_send.at[0, k], c_recv.at[0, k])

    def got_p(k):
        pc[k].wait_recv()
        o = (outer + outer_size - k) % outer_size
        block = index_of(o, first_mid, core, first_rep)
        dc[k] = send(block, second_dom, second_rep, d_send.at[k], d_recv.at[k])
        cc[1, k] = send(block, dom_core, rep, c_send.at[1, k], c_recv.at[1, k])

    def got_q(k):
        qc[k].wait_recv()
        o = (outer + outer_size - k) % outer_size
        second_mid = mid + core * (1 - 2 * mid)
        cc[2, k] = send(index_of(o, second_mid, core, second_rep), dom_core, rep, c_send.at[2, k], c_recv.at[2, k])

    def got_d(k):
        dc[k].wait_recv()
        o = (outer + outer_size - k) % outer_size
        cc[3, k] = send(index_of(o, 1 - mid, core, rep_other), dom_core, rep, c_send.at[3, k], c_recv.at[3, k])

    for k in range(1, outer_size):
        o = (outer + k) % outer_size
        zc[k] = send(me, o * 4 + dom % 4, rep, z_send.at[k - 1], z_recv.at[k - 1])
    column(0)

    for load in loads:
        load.wait()
    date_word = flag_ref[0:1, :]
    for j in range(1, flag_ref.shape[0]):
        date_word = date_word | (flag_ref[j : j + 1, :] << j)
    week_mul, week_shift = divider(week_length, flag_ref.shape[0] * LANES)
    dev_mul, dev_shift = divider(item_rows, item_rows * devices)
    count = count_ref[0]

    def prepare(g, carry):
        start = pl.multiple_of(g * 8, 8)
        rows = pl.ds(start, 8)
        date = date_v[rows, :]
        day = (lookup(date_word, date & (LANES - 1)) >> (date >> 7)) & 1
        store = store_v[rows, :]
        region = lookup(region_ref[0:1, :], store & (LANES - 1))
        for j in range(1, region_ref.shape[0]):
            region = jnp.where((store >> 7) == j, lookup(region_ref[j : j + 1, :], store & (LANES - 1)), region)
        slot = base + start + lax.broadcasted_iota(jnp.int32, (8, LANES), 0)
        ok = (day == 1) & (slot < count)
        reg_f[rows, :] = jnp.where(ok, region, -1).astype(jnp.float32)
        week_f[rows, :] = ((date * week_mul) >> week_shift).astype(jnp.float32)
        quantity = meas_v[pl.ds(start * 4, 8, stride=4), :]
        selling = meas_v[pl.ds(start * 4 + 1, 8, stride=4), :]
        wholesale = meas_v[pl.ds(start * 4 + 2, 8, stride=4), :]
        coupon = meas_v[pl.ds(start * 4 + 3, 8, stride=4), :]
        prof_f[rows, :] = quantity * (selling - wholesale) - coupon
        rev_f[rows, :] = quantity * selling - coupon
        qty_f[rows, :] = quantity
        item = item_v[rows, :]
        page = item >> 7
        holder = (page * dev_mul) >> dev_shift
        lane_i[rows, :] = item & (LANES - 1)
        row_i[rows, :] = (holder >> 5) * item_rows + page - holder * item_rows
        bit_i[rows, :] = holder & 31
        return carry

    lax.fori_loop(0, half // 8, prepare, 0)

    for k in range(outer_size):
        got_p(k)
        if k + 1 < outer_size:
            zc[k + 1].wait_recv()
            column(k + 1)
        got_q(k)
        if k >= 1:
            got_d(k - 1)
    got_d(outer_size - 1)
    for k in range(outer_size):
        for j in range(4):
            cc[j, k].wait_recv()

    for g in range((devices + 31) // 32):
        word = None
        for h in range(2):
            total = None
            for b in range(16):
                device = g * 32 + h * 16 + b
                if device < devices:
                    piece = flags[device].astype(jnp.float32)
                    total = piece if total is None else total + piece
            if total is not None:
                bits = total.astype(jnp.int32)
                word = bits if h == 0 else word | (bits << 16)
        words[g * item_rows : (g + 1) * item_rows, :] = word[:item_rows]

    acc[...] = jnp.zeros(acc.shape, jnp.float32)
    weeks = acc.shape[1]
    word_rows = words.shape[0]
    iota = lax.broadcasted_iota(jnp.int32, (16, LANES), 0).astype(jnp.float32)
    region_iota = [(iota + 16.0 * j).astype(jnp.bfloat16) for j in range(regions // 16)]
    week_iota = [(iota + 16.0 * j).astype(jnp.bfloat16) for j in range(weeks // 16)]
    zero = jnp.zeros((16, LANES), jnp.bfloat16)
    one = jnp.ones((16, LANES), jnp.bfloat16)

    def add_chunk(n, carry):
        first = pl.multiple_of(n * chunk, 8)
        for g in range(chunk // 8):
            rows = pl.ds(first + 8 * g, 8)
            lane, row = lane_i[rows, :], row_i[rows, :]
            found = lookup(words[0:1, :], lane)
            for w in range(1, word_rows):
                found = jnp.where(row == w, lookup(words[w : w + 1, :], lane), found)
            hit = (found >> bit_i[rows, :]) & 1
            reg_f[rows, :] = jnp.where(hit == 1, reg_f[rows, :], -1.0)
        lefts, rights = [], []
        for s in range(chunk):
            line = pl.ds(first + s, 1)

            def spread(ref):
                return jnp.broadcast_to(ref[line, :], (16, LANES)).astype(jnp.bfloat16)

            region, week = spread(reg_f), spread(week_f)
            values = [spread(prof_f), spread(rev_f), spread(qty_f)]
            masks = [one_iota == region for one_iota in region_iota]
            lefts.append(jnp.concatenate([jnp.where(m, v, zero) for v in values for m in masks], axis=0))
            rights.append(jnp.concatenate([jnp.where(w == week, one, zero) for w in week_iota], axis=0))
        left = jnp.concatenate(lefts, axis=1)
        right = jnp.concatenate(rights, axis=1)
        acc[...] += lax.dot_general(left, right, (((1,), (1,)), ((), ())), preferred_element_type=jnp.float32)
        return carry

    lax.fori_loop(0, half // chunk, add_chunk, 0)

    tile = fbuf.shape[1]
    tiles = fbuf.shape[0]
    cols = weeks // rep_size
    for j in range(rep_size):
        part[j] = acc[:, j * cols : (j + 1) * cols].astype(jnp.bfloat16)
    my_tile = (dom * tiles + dom_size - 1) // dom_size
    is_owner = jnp.logical_and(my_tile < tiles, (my_tile * dom_size) // tiles == dom)

    def partial_copy(t, j):
        owner = t * dom_size // tiles
        target = owner * rep_size + j
        slot = (me + devices - target) % devices
        return target, pltpu.make_async_remote_copy(
            src_ref=part.at[j, pl.ds(t * tile, tile)], dst_ref=rbuf.at[slot],
            send_sem=r_send.at[t, j], recv_sem=r_recv.at[slot],
            device_id={"dom": owner, "rep": j}, device_id_type=MESH,
        )

    for t in range(tiles):
        for j in range(rep_size):
            target, copy = partial_copy(t, j)

            @pl.when(target != me)
            def _():
                copy.start()

    def final_copy(k):
        other = (dom + k) % dom_size
        return pltpu.make_async_remote_copy(
            src_ref=fbuf.at[my_tile], dst_ref=fbuf.at[my_tile],
            send_sem=f_send.at[k], recv_sem=f_recv.at[my_tile],
            device_id={"dom": other, "rep": rep}, device_id_type=MESH,
        )

    @pl.when(is_owner)
    def _():
        total = part[rep, pl.ds(pl.multiple_of(my_tile * tile, tile), tile), :].astype(jnp.float32)
        for slot in range(1, devices):
            pltpu.make_async_copy(rbuf.at[slot], rbuf.at[slot], r_recv.at[slot]).wait()
            total = total + rbuf[slot].astype(jnp.float32)
        fbuf[my_tile] = total
        for k in range(1, dom_size):
            final_copy(k).start()

    for t in range(tiles):

        @pl.when(jnp.logical_not(jnp.logical_and(is_owner, my_tile == t)))
        def _():
            pltpu.make_async_copy(fbuf.at[t], fbuf.at[t], f_recv.at[t]).wait()

    out_ref[...] = fbuf[...]

    @pl.when(is_owner)
    def _():
        for k in range(1, dom_size):
            final_copy(k).wait_send()

    for t in range(tiles):
        for j in range(rep_size):
            target, copy = partial_copy(t, j)

            @pl.when(target != me)
            def _():
                copy.wait_send()

    for copy in sends:
        copy.wait_send()


def per_device(
    date_key, item_key, store_key, measures, block_count, item_price, store_region, date_flag
):
    dom_size = lax.axis_size("dom")
    rep_size = lax.axis_size("rep")
    devices = dom_size * rep_size
    regions = REG_DEV * dom_size
    weeks = date_flag.shape[0] // week_length
    slots = date_key.shape[0]
    half = slots // rep_size
    item_rows = item_price.shape[0] // LANES
    chunk = 16
    tile = 16
    tiles = AGGS * regions // tile
    outer = dom_size // 4
    bf16, f32, i32 = jnp.bfloat16, jnp.float32, jnp.int32
    dma = pltpu.SemaphoreType.DMA
    vmem = pl.BlockSpec(memory_space=pltpu.VMEM)
    hbm = pl.BlockSpec(memory_space=pl.ANY)
    facts = (half, LANES)
    out = pl.pallas_call(
        functools.partial(kernel, dom_size, rep_size, regions, item_rows, slots, chunk),
        out_shape=jax.ShapeDtypeStruct((tiles, tile, weeks // rep_size), f32),
        in_specs=[pl.BlockSpec(memory_space=pltpu.SMEM), hbm, hbm, hbm, hbm, vmem, vmem, vmem],
        out_specs=vmem,
        scratch_shapes=[
            pltpu.VMEM(facts, i32), pltpu.VMEM(facts, i32), pltpu.VMEM(facts, i32),
            pltpu.VMEM((half * 4, LANES), f32),
            pltpu.VMEM((devices, round_up(item_rows, 16), LANES), bf16),
            pltpu.VMEM(((devices + 31) // 32 * item_rows, LANES), i32),
            pltpu.VMEM(facts, f32), pltpu.VMEM(facts, f32), pltpu.VMEM(facts, f32),
            pltpu.VMEM(facts, f32), pltpu.VMEM(facts, f32),
            pltpu.VMEM(facts, i32), pltpu.VMEM(facts, i32), pltpu.VMEM(facts, i32),
            pltpu.VMEM((AGGS * regions, weeks), f32),
            pltpu.VMEM((rep_size, AGGS * regions, weeks // rep_size), bf16),
            pltpu.VMEM((devices, tile, weeks // rep_size), bf16),
            pltpu.VMEM((tiles, tile, weeks // rep_size), f32),
            dma((4,)),
            dma((outer - 1,)), dma((outer - 1,)),
            dma((outer,)), dma((outer,)), dma((outer,)), dma((outer,)), dma((outer,)), dma((outer,)),
            dma((4, outer)), dma((4, outer)),
            dma((tiles, rep_size)), dma((devices,)),
            dma((dom_size,)), dma((tiles,)),
        ],
        compiler_params=pltpu.CompilerParams(
            collective_id=0, has_side_effects=True, vmem_limit_bytes=40 * 1024 * 1024
        ),
        cost_estimate=pl.CostEstimate(
            flops=2 * AGGS * regions * weeks * half * LANES, bytes_accessed=half * LANES * 28, transcendentals=0
        ),
    )(
        block_count, date_key, item_key, store_key, measures.reshape(slots * 4, LANES),
        item_price.reshape(item_rows, LANES), store_region.reshape(-1, LANES), date_flag.reshape(-1, LANES),
    )
    return out.reshape(AGGS, regions, weeks // rep_size)


def solution(mesh):
    placed = (
        P("dom", None),
        P("dom", None),
        P("dom", None),
        P("dom", None, None),
        P("dom"),
        P(("dom", "rep")),
        P(),
        P(),
    )
    return jax.shard_map(
        per_device, mesh=mesh, in_specs=placed, out_specs=P(None, None, "rep"), check_vma=False
    )
```

```python
import functools

import jax
import jax.numpy as jnp
import numpy as np
from jax import lax
from jax.experimental import pallas as pl
from jax.experimental.pallas import tpu as pltpu
from jax.sharding import PartitionSpec as P

MESH = pl.DeviceIdType.MESH
AGGS = 3
REG_DEV = 2
LANES = 128
low_price = 0.2
high_price = 0.8
week_length = 7


def round_up(value, step):
    return (value + step - 1) // step * step


def divider(divisor, limit):
    n = np.arange(limit, dtype=np.int64)
    for shift in range(8, 24):
        multiplier = -(-(1 << shift) // divisor)
        if (limit * multiplier) < (1 << 31) and np.array_equal((n * multiplier) >> shift, n // divisor):
            return multiplier, shift
    raise ValueError("no divider")


def lookup(row, lane):
    return jnp.take_along_axis(jnp.broadcast_to(row, lane.shape), lane, axis=1)


def kernel(
    dom_size, rep_size, regions, item_rows, slots, chunk,
    count_ref, date_hbm, item_hbm, store_hbm, meas_hbm, price_hbm, region_hbm, flag_hbm,
    out_ref,
    date_v, item_v, store_v, meas_v, price_ref, region_ref, flag_ref,
    flags, words, reg_f, hit_f, week_f, prof_f, rev_f, qty_f, lane_i, row_i, bit_i, week_hot,
    acc, part, rbuf, fbuf,
    in_sem, z_send, z_recv, p_send, p_recv, q_send, q_recv, d_send, d_recv, c_send, c_recv,
    r_send, r_recv, f_send, f_recv,
):
    dom = lax.axis_index("dom")
    rep = lax.axis_index("rep")
    devices = dom_size * rep_size
    me = dom * rep_size + rep
    half = slots // rep_size
    outer_size = dom_size // 4
    outer = dom // 4
    mid = (dom // 2) % 2
    core = dom % 2

    base = pl.multiple_of(rep * half, 8)
    price_load = pltpu.make_async_copy(price_hbm, price_ref, in_sem.at[4])
    price_load.start()
    loads = [
        pltpu.make_async_copy(date_hbm.at[pl.ds(base, half)], date_v, in_sem.at[0]),
        pltpu.make_async_copy(item_hbm.at[pl.ds(base, half)], item_v, in_sem.at[1]),
        pltpu.make_async_copy(store_hbm.at[pl.ds(base, half)], store_v, in_sem.at[2]),
        pltpu.make_async_copy(meas_hbm.at[pl.ds(base * 4, half * 4)], meas_v, in_sem.at[3]),
        pltpu.make_async_copy(region_hbm, region_ref, in_sem.at[5]),
        pltpu.make_async_copy(flag_hbm, flag_ref, in_sem.at[6]),
    ]
    for load in loads:
        load.start()

    barrier = pltpu.get_barrier_semaphore()
    for k in range(1, devices):
        other = (me + k) % devices
        pl.semaphore_signal(
            barrier, inc=1, device_id={"dom": other // rep_size, "rep": other % rep_size}, device_id_type=MESH
        )

    padded = flags.shape[1]
    price_load.wait()
    price = price_ref[...]
    power = jnp.left_shift(jnp.ones(price.shape, jnp.int32), me % 16).astype(jnp.float32)
    mark = jnp.where((price >= low_price) & (price <= high_price), power, 0.0)
    if padded > item_rows:
        mark = jnp.concatenate([mark, jnp.zeros((padded - item_rows, LANES), jnp.float32)], axis=0)
    flags[me] = mark.astype(jnp.bfloat16)
    pl.semaphore_wait(barrier, devices - 1)

    def index_of(o, m, c, r):
        return ((o * 2 + m) * 2 + c) * rep_size + r

    sends = []

    def send(block, to_dom, to_rep, s_sem, r_sem):
        copy = pltpu.make_async_remote_copy(
            src_ref=flags.at[block], dst_ref=flags.at[block], send_sem=s_sem, recv_sem=r_sem,
            device_id={"dom": to_dom, "rep": to_rep}, device_id_type=MESH,
        )
        copy.start()
        sends.append(copy)
        return copy

    dom_mid = dom + 2 - 4 * mid
    rep_other = (rep + 1) % rep_size
    dom_core = dom + 1 - 2 * core
    first_dom, first_rep = dom + (1 - core) * (2 - 4 * mid), rep + core * (rep_other - rep)
    second_dom, second_rep = dom + core * (2 - 4 * mid), rep + (1 - core) * (rep_other - rep)
    first_mid = mid + (1 - core) * (1 - 2 * mid)

    zc, pc, qc, dc, cc = {}, {}, {}, {}, {}

    def column(k):
        o = (outer + outer_size - k) % outer_size
        block = index_of(o, mid, core, rep)
        pc[k] = send(block, first_dom, first_rep, p_send.at[k], p_recv.at[k])
        qc[k] = send(block, second_dom, second_rep, q_send.at[k], q_recv.at[k])
        cc[0, k] = send(block, dom_core, rep, c_send.at[0, k], c_recv.at[0, k])

    def got_p(k):
        pc[k].wait_recv()
        o = (outer + outer_size - k) % outer_size
        block = index_of(o, first_mid, core, first_rep)
        dc[k] = send(block, second_dom, second_rep, d_send.at[k], d_recv.at[k])
        cc[1, k] = send(block, dom_core, rep, c_send.at[1, k], c_recv.at[1, k])

    def got_q(k):
        qc[k].wait_recv()
        o = (outer + outer_size - k) % outer_size
        second_mid = mid + core * (1 - 2 * mid)
        cc[2, k] = send(index_of(o, second_mid, core, second_rep), dom_core, rep, c_send.at[2, k], c_recv.at[2, k])

    def got_d(k):
        dc[k].wait_recv()
        o = (outer + outer_size - k) % outer_size
        cc[3, k] = send(index_of(o, 1 - mid, core, rep_other), dom_core, rep, c_send.at[3, k], c_recv.at[3, k])

    for k in range(1, outer_size):
        o = (outer + k) % outer_size
        zc[k] = send(me, o * 4 + dom % 4, rep, z_send.at[k - 1], z_recv.at[k - 1])
    column(0)

    for load in loads:
        load.wait()
    date_word = flag_ref[0:1, :]
    for j in range(1, flag_ref.shape[0]):
        date_word = date_word | (flag_ref[j : j + 1, :] << j)
    week_mul, week_shift = divider(week_length, flag_ref.shape[0] * LANES)
    dev_mul, dev_shift = divider(item_rows, item_rows * devices)
    count = count_ref[0]
    cols = week_hot.shape[1]
    mid_group = regions * rep_size // 2

    def prepare(g, carry):
        start = pl.multiple_of(g * 8, 8)
        rows = pl.ds(start, 8)
        date = date_v[rows, :]
        day = (lookup(date_word, date & (LANES - 1)) >> (date >> 7)) & 1
        store = store_v[rows, :]
        region = lookup(region_ref[0:1, :], store & (LANES - 1))
        for j in range(1, region_ref.shape[0]):
            region = jnp.where((store >> 7) == j, lookup(region_ref[j : j + 1, :], store & (LANES - 1)), region)
        slot = base + start + lax.broadcasted_iota(jnp.int32, (8, LANES), 0)
        ok = (day == 1) & (slot < count)
        week = (date * week_mul) >> week_shift
        part_of = jnp.zeros(week.shape, jnp.int32)
        for j in range(1, rep_size):
            part_of = jnp.where(week >= j * cols, j, part_of)
        reg_f[rows, :] = jnp.where(ok, part_of * regions + region - mid_group, mid_group).astype(jnp.float32)
        week_f[rows, :] = (week - part_of * cols).astype(jnp.float32)
        quantity = meas_v[pl.ds(start * 4, 8, stride=4), :]
        selling = meas_v[pl.ds(start * 4 + 1, 8, stride=4), :]
        wholesale = meas_v[pl.ds(start * 4 + 2, 8, stride=4), :]
        coupon = meas_v[pl.ds(start * 4 + 3, 8, stride=4), :]
        prof_f[rows, :] = quantity * (selling - wholesale) - coupon
        rev_f[rows, :] = quantity * selling - coupon
        qty_f[rows, :] = quantity
        item = item_v[rows, :]
        page = item >> 7
        holder = (page * dev_mul) >> dev_shift
        lane_i[rows, :] = item & (LANES - 1)
        row_i[rows, :] = (holder >> 5) * item_rows + page - holder * item_rows
        bit_i[rows, :] = holder & 31
        return carry

    lax.fori_loop(0, half // 8, prepare, 0)

    column_iota = lax.broadcasted_iota(jnp.int32, (LANES, cols), 1).astype(jnp.float32)

    def build_weeks(n):
        turned = jnp.transpose(week_f[n * chunk : (n + 1) * chunk, :])
        for i in range(chunk):
            hot = jnp.where(turned[:, i : i + 1] == column_iota, 1.0, 0.0).astype(jnp.bfloat16)
            week_hot[(n * chunk + i) * LANES : (n * chunk + i + 1) * LANES, :] = hot

    chunks = half // chunk
    to_build = list(range(chunks))

    def idle():
        if to_build:
            build_weeks(to_build.pop(0))

    for k in range(outer_size):
        got_p(k)
        idle()
        if k + 1 < outer_size:
            zc[k + 1].wait_recv()
            column(k + 1)
            idle()
        got_q(k)
        idle()
        if k >= 1:
            got_d(k - 1)
    got_d(outer_size - 1)
    while to_build:
        idle()
    for k in range(outer_size):
        for j in range(4):
            cc[j, k].wait_recv()

    for g in range((devices + 31) // 32):
        word = None
        for h in range(2):
            total = None
            for b in range(16):
                device = g * 32 + h * 16 + b
                if device < devices:
                    piece = flags[device].astype(jnp.float32)
                    total = piece if total is None else total + piece
            if total is not None:
                bits = total.astype(jnp.int32)
                word = bits if h == 0 else word | (bits << 16)
        words[g * item_rows : (g + 1) * item_rows, :] = word[:item_rows]

    acc[...] = jnp.zeros(acc.shape, jnp.float32)
    word_rows = words.shape[0]
    groups = regions * rep_size
    iota = lax.broadcasted_iota(jnp.int32, (16, LANES), 0).astype(jnp.float32)
    group_iota = [(iota + (16.0 * j - mid_group)).astype(jnp.bfloat16) for j in range(groups // 16)]
    per_part = regions // 16
    zero = jnp.zeros((16, LANES), jnp.bfloat16)

    def hits(n):
        first = pl.multiple_of(n * chunk, 8)
        found_all = []
        for g in range(chunk // 8):
            rows = pl.ds(first + 8 * g, 8)
            lane, row = lane_i[rows, :], row_i[rows, :]
            found = lookup(words[0:1, :], lane)
            for w in range(1, word_rows):
                found = jnp.where(row == w, lookup(words[w : w + 1, :], lane), found)
            hit = (found >> bit_i[rows, :]) & 1
            found_all.append(jnp.where(hit == 1, reg_f[rows, :], float(mid_group)))
        return found_all

    def put(slot, found_all):
        for g in range(chunk // 8):
            hit_f[slot, 8 * g : 8 * g + 8, :] = found_all[g]

    put(0, hits(0))

    def add_chunk(n, carry):
        first = pl.multiple_of(n * chunk, 8)
        ahead = hits(jnp.minimum(n + 1, chunks - 1))
        lefts = []
        for i in range(chunk):

            def spread(row):
                return jnp.broadcast_to(row, (16, LANES)).astype(jnp.bfloat16)

            group = spread(hit_f[n % 2, i : i + 1, :])
            line = pl.ds(first + i, 1)
            values = [spread(prof_f[line, :]), spread(rev_f[line, :]), spread(qty_f[line, :])]
            masks = [one_iota == group for one_iota in group_iota]
            lefts.append(
                jnp.concatenate(
                    [
                        jnp.where(m, v, zero)
                        for j in range(rep_size)
                        for v in values
                        for m in masks[j * per_part : (j + 1) * per_part]
                    ],
                    axis=0,
                )
            )
        left = jnp.concatenate(lefts, axis=1)
        right = week_hot[pl.ds(pl.multiple_of(first * LANES, LANES), chunk * LANES), :]
        acc[...] += jnp.dot(left, right, preferred_element_type=jnp.float32)
        put((n + 1) % 2, ahead)
        return carry

    lax.fori_loop(0, chunks, add_chunk, 0)

    tile = fbuf.shape[1]
    tiles = fbuf.shape[0]
    out_rows = AGGS * regions
    for j in range(rep_size):
        part[j] = acc[j * out_rows : (j + 1) * out_rows, :].astype(jnp.bfloat16)
    my_tile = (dom * tiles + dom_size - 1) // dom_size
    is_owner = jnp.logical_and(my_tile < tiles, (my_tile * dom_size) // tiles == dom)

    def partial_copy(t, j):
        owner = t * dom_size // tiles
        target = owner * rep_size + j
        slot = (me + devices - target) % devices
        return target, pltpu.make_async_remote_copy(
            src_ref=part.at[j, pl.ds(t * tile, tile)], dst_ref=rbuf.at[slot],
            send_sem=r_send.at[t, j], recv_sem=r_recv.at[slot],
            device_id={"dom": owner, "rep": j}, device_id_type=MESH,
        )

    for t in range(tiles):
        for j in range(rep_size):
            target, copy = partial_copy(t, j)

            @pl.when(target != me)
            def _():
                copy.start()

    def final_copy(k):
        other = (dom + k) % dom_size
        return pltpu.make_async_remote_copy(
            src_ref=fbuf.at[my_tile], dst_ref=fbuf.at[my_tile],
            send_sem=f_send.at[k], recv_sem=f_recv.at[my_tile],
            device_id={"dom": other, "rep": rep}, device_id_type=MESH,
        )

    @pl.when(is_owner)
    def _():
        total = part[rep, pl.ds(pl.multiple_of(my_tile * tile, tile), tile), :].astype(jnp.float32)
        for slot in range(1, devices):
            pltpu.make_async_copy(rbuf.at[slot], rbuf.at[slot], r_recv.at[slot]).wait()
            total = total + rbuf[slot].astype(jnp.float32)
        fbuf[my_tile] = total
        for k in range(1, dom_size):
            final_copy(k).start()

    for t in range(tiles):

        @pl.when(jnp.logical_not(jnp.logical_and(is_owner, my_tile == t)))
        def _():
            pltpu.make_async_copy(fbuf.at[t], fbuf.at[t], f_recv.at[t]).wait()

    out_ref[...] = fbuf[...]

    @pl.when(is_owner)
    def _():
        for k in range(1, dom_size):
            final_copy(k).wait_send()

    for t in range(tiles):
        for j in range(rep_size):
            target, copy = partial_copy(t, j)

            @pl.when(target != me)
            def _():
                copy.wait_send()

    for copy in sends:
        copy.wait_send()


def per_device(
    date_key, item_key, store_key, measures, block_count, item_price, store_region, date_flag
):
    dom_size = lax.axis_size("dom")
    rep_size = lax.axis_size("rep")
    devices = dom_size * rep_size
    regions = REG_DEV * dom_size
    weeks = date_flag.shape[0] // week_length
    slots = date_key.shape[0]
    half = slots // rep_size
    item_rows = item_price.shape[0] // LANES
    chunk = 16
    tile = 16
    tiles = AGGS * regions // tile
    outer = dom_size // 4
    bf16, f32, i32 = jnp.bfloat16, jnp.float32, jnp.int32
    dma = pltpu.SemaphoreType.DMA
    vmem = pl.BlockSpec(memory_space=pltpu.VMEM)
    hbm = pl.BlockSpec(memory_space=pl.ANY)
    facts = (half, LANES)
    out = pl.pallas_call(
        functools.partial(kernel, dom_size, rep_size, regions, item_rows, slots, chunk),
        out_shape=jax.ShapeDtypeStruct((tiles, tile, weeks // rep_size), f32),
        in_specs=[pl.BlockSpec(memory_space=pltpu.SMEM), hbm, hbm, hbm, hbm, hbm, hbm, hbm],
        out_specs=vmem,
        scratch_shapes=[
            pltpu.VMEM(facts, i32), pltpu.VMEM(facts, i32), pltpu.VMEM(facts, i32),
            pltpu.VMEM((half * 4, LANES), f32),
            pltpu.VMEM((item_rows, LANES), f32),
            pltpu.VMEM((store_region.shape[0] // LANES, LANES), i32),
            pltpu.VMEM((date_flag.shape[0] // LANES, LANES), i32),
            pltpu.VMEM((devices, round_up(item_rows, 16), LANES), bf16),
            pltpu.VMEM(((devices + 31) // 32 * item_rows, LANES), i32),
            pltpu.VMEM(facts, f32), pltpu.VMEM((2, chunk, LANES), f32),
            pltpu.VMEM(facts, f32), pltpu.VMEM(facts, f32), pltpu.VMEM(facts, f32), pltpu.VMEM(facts, f32),
            pltpu.VMEM(facts, i32), pltpu.VMEM(facts, i32), pltpu.VMEM(facts, i32),
            pltpu.VMEM((half * LANES, weeks // rep_size), bf16),
            pltpu.VMEM((rep_size * AGGS * regions, weeks // rep_size), f32),
            pltpu.VMEM((rep_size, AGGS * regions, weeks // rep_size), bf16),
            pltpu.VMEM((devices, tile, weeks // rep_size), bf16),
            pltpu.VMEM((tiles, tile, weeks // rep_size), f32),
            dma((7,)),
            dma((outer - 1,)), dma((outer - 1,)),
            dma((outer,)), dma((outer,)), dma((outer,)), dma((outer,)), dma((outer,)), dma((outer,)),
            dma((4, outer)), dma((4, outer)),
            dma((tiles, rep_size)), dma((devices,)),
            dma((dom_size,)), dma((tiles,)),
        ],
        compiler_params=pltpu.CompilerParams(
            collective_id=0, has_side_effects=True, vmem_limit_bytes=60 * 1024 * 1024
        ),
        cost_estimate=pl.CostEstimate(
            flops=2 * AGGS * regions * weeks * half * LANES, bytes_accessed=half * LANES * 28, transcendentals=0
        ),
    )(
        block_count, date_key, item_key, store_key, measures.reshape(slots * 4, LANES),
        item_price.reshape(item_rows, LANES), store_region.reshape(-1, LANES), date_flag.reshape(-1, LANES),
    )
    return out.reshape(AGGS, regions, weeks // rep_size)


def solution(mesh):
    placed = (
        P("dom", None),
        P("dom", None),
        P("dom", None),
        P("dom", None, None),
        P("dom"),
        P(("dom", "rep")),
        P(),
        P(),
    )
    return jax.shard_map(
        per_device, mesh=mesh, in_specs=placed, out_specs=P(None, None, "rep"), check_vma=False
    )
```

```python
import functools

import jax
import jax.numpy as jnp
import numpy as np
from jax import lax
from jax.experimental import pallas as pl
from jax.experimental.pallas import tpu as pltpu
from jax.sharding import PartitionSpec as P

MESH = pl.DeviceIdType.MESH
AGGS = 3
REG_DEV = 2
LANES = 128
low_price = 0.2
high_price = 0.8
week_length = 7


def round_up(value, step):
    return (value + step - 1) // step * step


def divider(divisor, limit):
    n = np.arange(limit, dtype=np.int64)
    for shift in range(8, 24):
        multiplier = -(-(1 << shift) // divisor)
        if (limit * multiplier) < (1 << 31) and np.array_equal((n * multiplier) >> shift, n // divisor):
            return multiplier, shift
    raise ValueError("no divider")


def lookup(row, lane):
    return jnp.take_along_axis(jnp.broadcast_to(row, lane.shape), lane, axis=1)


def kernel(
    dom_size, rep_size, regions, item_rows, slots, chunk,
    count_ref, date_hbm, item_hbm, store_hbm, meas_hbm, price_hbm, region_hbm, flag_hbm,
    out_ref,
    date_v, item_v, store_v, meas_v, price_ref, region_ref, flag_ref,
    flags, words, reg_f, week_f, prof_f, rev_f, qty_f, lane_i, row_i, bit_i, found_i, left_hot,
    acc, part, rbuf, fbuf,
    in_sem, z_send, z_recv, p_send, p_recv, q_send, q_recv, d_send, d_recv, c_send, c_recv,
    r_send, r_recv, f_send, f_recv,
):
    dom = lax.axis_index("dom")
    rep = lax.axis_index("rep")
    devices = dom_size * rep_size
    me = dom * rep_size + rep
    half = slots // rep_size
    outer_size = dom_size // 4
    outer = dom // 4
    mid = (dom // 2) % 2
    core = dom % 2

    base = pl.multiple_of(rep * half, 8)
    price_load = pltpu.make_async_copy(price_hbm, price_ref, in_sem.at[4])
    price_load.start()
    loads = [
        pltpu.make_async_copy(date_hbm.at[pl.ds(base, half)], date_v, in_sem.at[0]),
        pltpu.make_async_copy(item_hbm.at[pl.ds(base, half)], item_v, in_sem.at[1]),
        pltpu.make_async_copy(store_hbm.at[pl.ds(base, half)], store_v, in_sem.at[2]),
        pltpu.make_async_copy(meas_hbm.at[pl.ds(base * 4, half * 4)], meas_v, in_sem.at[3]),
        pltpu.make_async_copy(region_hbm, region_ref, in_sem.at[5]),
        pltpu.make_async_copy(flag_hbm, flag_ref, in_sem.at[6]),
    ]
    for load in loads:
        load.start()

    barrier = pltpu.get_barrier_semaphore()
    for k in range(1, devices):
        other = (me + k) % devices
        pl.semaphore_signal(
            barrier, inc=1, device_id={"dom": other // rep_size, "rep": other % rep_size}, device_id_type=MESH
        )

    padded = flags.shape[1]
    price_load.wait()
    price = price_ref[...]
    shards = 4 * rep_size
    bands = padded // 16
    row_of = lax.broadcasted_iota(jnp.int32, price.shape, 0)
    place = ((me % shards) * bands + (row_of >> 4)) & 15
    power = jnp.left_shift(jnp.ones(price.shape, jnp.int32), place).astype(jnp.float32)
    mark = jnp.where((price >= low_price) & (price <= high_price), power, 0.0)
    if padded > item_rows:
        mark = jnp.concatenate([mark, jnp.zeros((padded - item_rows, LANES), jnp.float32)], axis=0)
    flags[me] = mark.astype(jnp.bfloat16)
    pl.semaphore_wait(barrier, devices - 1)

    def index_of(o, m, c, r):
        return ((o * 2 + m) * 2 + c) * rep_size + r

    sends = []

    def send(block, to_dom, to_rep, s_sem, r_sem):
        copy = pltpu.make_async_remote_copy(
            src_ref=flags.at[block], dst_ref=flags.at[block], send_sem=s_sem, recv_sem=r_sem,
            device_id={"dom": to_dom, "rep": to_rep}, device_id_type=MESH,
        )
        copy.start()
        sends.append(copy)
        return copy

    dom_mid = dom + 2 - 4 * mid
    rep_other = (rep + 1) % rep_size
    dom_core = dom + 1 - 2 * core
    first_dom, first_rep = dom + (1 - core) * (2 - 4 * mid), rep + core * (rep_other - rep)
    second_dom, second_rep = dom + core * (2 - 4 * mid), rep + (1 - core) * (rep_other - rep)
    first_mid = mid + (1 - core) * (1 - 2 * mid)

    zc, pc, qc, dc, cc = {}, {}, {}, {}, {}

    def column(k):
        o = (outer + outer_size - k) % outer_size
        block = index_of(o, mid, core, rep)
        pc[k] = send(block, first_dom, first_rep, p_send.at[k], p_recv.at[k])
        qc[k] = send(block, second_dom, second_rep, q_send.at[k], q_recv.at[k])
        cc[0, k] = send(block, dom_core, rep, c_send.at[0, k], c_recv.at[0, k])

    def got_p(k):
        pc[k].wait_recv()
        o = (outer + outer_size - k) % outer_size
        block = index_of(o, first_mid, core, first_rep)
        dc[k] = send(block, second_dom, second_rep, d_send.at[k], d_recv.at[k])
        cc[1, k] = send(block, dom_core, rep, c_send.at[1, k], c_recv.at[1, k])

    def got_q(k):
        qc[k].wait_recv()
        o = (outer + outer_size - k) % outer_size
        second_mid = mid + core * (1 - 2 * mid)
        cc[2, k] = send(index_of(o, second_mid, core, second_rep), dom_core, rep, c_send.at[2, k], c_recv.at[2, k])

    def got_d(k):
        dc[k].wait_recv()
        o = (outer + outer_size - k) % outer_size
        cc[3, k] = send(index_of(o, 1 - mid, core, rep_other), dom_core, rep, c_send.at[3, k], c_recv.at[3, k])

    for k in range(1, outer_size):
        o = (outer + k) % outer_size
        zc[k] = send(me, o * 4 + dom % 4, rep, z_send.at[k - 1], z_recv.at[k - 1])
    column(0)

    for load in loads:
        load.wait()
    date_word = flag_ref[0:1, :]
    for j in range(1, flag_ref.shape[0]):
        date_word = date_word | (flag_ref[j : j + 1, :] << j)
    week_mul, week_shift = divider(week_length, flag_ref.shape[0] * LANES)
    shard_mul, shard_shift = divider(shards, devices)
    dev_mul, dev_shift = divider(item_rows, item_rows * devices)
    count = count_ref[0]
    cols = acc.shape[1]
    mid_group = regions * rep_size // 2

    def prepare(g, carry):
        start = pl.multiple_of(g * 8, 8)
        rows = pl.ds(start, 8)
        date = date_v[rows, :]
        day = (lookup(date_word, date & (LANES - 1)) >> (date >> 7)) & 1
        store = store_v[rows, :]
        region = lookup(region_ref[0:1, :], store & (LANES - 1))
        for j in range(1, region_ref.shape[0]):
            region = jnp.where((store >> 7) == j, lookup(region_ref[j : j + 1, :], store & (LANES - 1)), region)
        slot = base + start + lax.broadcasted_iota(jnp.int32, (8, LANES), 0)
        ok = (day == 1) & (slot < count)
        week = (date * week_mul) >> week_shift
        part_of = jnp.zeros(week.shape, jnp.int32)
        for j in range(1, rep_size):
            part_of = jnp.where(week >= j * cols, j, part_of)
        reg_f[rows, :] = jnp.where(ok, part_of * regions + region - mid_group, mid_group).astype(jnp.float32)
        week_f[rows, :] = (week - part_of * cols).astype(jnp.float32)
        quantity = meas_v[pl.ds(start * 4, 8, stride=4), :]
        selling = meas_v[pl.ds(start * 4 + 1, 8, stride=4), :]
        wholesale = meas_v[pl.ds(start * 4 + 2, 8, stride=4), :]
        coupon = meas_v[pl.ds(start * 4 + 3, 8, stride=4), :]
        prof_f[rows, :] = quantity * (selling - wholesale) - coupon
        rev_f[rows, :] = quantity * selling - coupon
        qty_f[rows, :] = quantity
        item = item_v[rows, :]
        page = item >> 7
        holder = (page * dev_mul) >> dev_shift
        lane_i[rows, :] = item & (LANES - 1)
        row = page - holder * item_rows
        far = (holder * shard_mul) >> shard_shift
        row_i[rows, :] = far * 16 + (row & 15)
        bit_i[rows, :] = (holder - far * shards) * bands + (row >> 4)
        found_i[rows, :] = jnp.zeros((8, LANES), jnp.int32)
        return carry

    lax.fori_loop(0, half // 8, prepare, 0)

    groups = regions * rep_size
    iota = lax.broadcasted_iota(jnp.int32, (16, LANES), 0).astype(jnp.float32)
    group_iota = [(iota + (16.0 * j - mid_group)).astype(jnp.bfloat16) for j in range(groups // 16)]
    week_iota = [(iota + 16.0 * j).astype(jnp.bfloat16) for j in range(cols // 16)]
    per_part = regions // 16
    zero = jnp.zeros((16, LANES), jnp.bfloat16)
    one = jnp.ones((16, LANES), jnp.bfloat16)
    chunks = half // chunk
    prebuilt = left_hot.shape[0] == chunks

    def spread(ref, line):
        return jnp.broadcast_to(ref[line, :], (16, LANES)).astype(jnp.bfloat16)

    def left_tiles(line):
        group = spread(reg_f, line)
        values = [spread(prof_f, line), spread(rev_f, line), spread(qty_f, line)]
        masks = [one_iota == group for one_iota in group_iota]
        return [
            jnp.where(m, v, zero)
            for j in range(rep_size)
            for v in values
            for m in masks[j * per_part : (j + 1) * per_part]
        ]

    def build_left(n, at):
        for i in range(chunk):
            tiles_of = left_tiles(pl.ds(n * chunk + i, 1))
            for j, values in enumerate(tiles_of):
                left_hot[at, 16 * j : 16 * j + 16, i * LANES : (i + 1) * LANES] = values

    to_build = list(range(chunks)) if prebuilt else []

    def idle(amount=1):
        for _ in range(amount):
            if to_build:
                n = to_build.pop(0)
                build_left(n, n)

    word_rows = min(16, item_rows)

    def look_up(k):
        for j in range(4):
            cc[j, k].wait_recv()
        o = (outer + outer_size - k) % outer_size
        halves = [None, None]
        for s in range(shards):
            for q in range(bands):
                piece = flags[o * shards + s, 16 * q : 16 * q + 16, :].astype(jnp.float32)
                h = (s * bands + q) // 16
                halves[h] = piece if halves[h] is None else halves[h] + piece
        word = halves[0].astype(jnp.int32)
        if halves[1] is not None:
            word = word | (halves[1].astype(jnp.int32) << 16)
        words[k % 2] = word

        def look(g, carry):
            for u in range(2):
                rows = pl.ds(pl.multiple_of(g * 16 + 8 * u, 8), 8)
                lane, row = lane_i[rows, :], row_i[rows, :] - o * 16
                found = found_i[rows, :]
                for w in range(word_rows):
                    found = jnp.where(row == w, lookup(words[k % 2, w : w + 1, :], lane), found)
                found_i[rows, :] = found
            return carry

        lax.fori_loop(0, half // 16, look, 0)

    for k in range(outer_size):
        got_p(k)
        idle()
        if k + 1 < outer_size:
            zc[k + 1].wait_recv()
            column(k + 1)
            idle()
        got_q(k)
        idle()
        got_d(k)
        if k >= 1:
            look_up(k - 1)
    idle(chunks)
    look_up(outer_size - 1)

    acc[...] = jnp.zeros(acc.shape, jnp.float32)

    def add_chunk(n, carry):
        first = pl.multiple_of(n * chunk, 8)
        for g in range(chunk // 8):
            rows = pl.ds(first + 8 * g, 8)
            hit = (found_i[rows, :] >> bit_i[rows, :]) & 1
            week_f[rows, :] = jnp.where(hit == 1, week_f[rows, :], -1.0)
        rights = []
        for i in range(chunk):
            week = spread(week_f, pl.ds(first + i, 1))
            rights.append(jnp.concatenate([jnp.where(w == week, one, zero) for w in week_iota], axis=0))
        right = jnp.concatenate(rights, axis=1)
        if not prebuilt:
            build_left(n, 0)
        left = left_hot[n if prebuilt else 0]
        acc[...] += lax.dot_general(left, right, (((1,), (1,)), ((), ())), preferred_element_type=jnp.float32)
        return carry

    lax.fori_loop(0, chunks, add_chunk, 0)

    tile = fbuf.shape[1]
    tiles = fbuf.shape[0]
    out_rows = AGGS * regions
    for j in range(rep_size):
        part[j] = acc[j * out_rows : (j + 1) * out_rows, :].astype(jnp.bfloat16)
    my_tile = (dom * tiles + dom_size - 1) // dom_size
    is_owner = jnp.logical_and(my_tile < tiles, (my_tile * dom_size) // tiles == dom)

    def partial_copy(t, j):
        owner = t * dom_size // tiles
        target = owner * rep_size + j
        slot = (me + devices - target) % devices
        return target, pltpu.make_async_remote_copy(
            src_ref=part.at[j, pl.ds(t * tile, tile)], dst_ref=rbuf.at[slot],
            send_sem=r_send.at[t, j], recv_sem=r_recv.at[slot],
            device_id={"dom": owner, "rep": j}, device_id_type=MESH,
        )

    for t in range(tiles):
        for j in range(rep_size):
            target, copy = partial_copy(t, j)

            @pl.when(target != me)
            def _():
                copy.start()

    def final_copy(k):
        other = (dom + k) % dom_size
        return pltpu.make_async_remote_copy(
            src_ref=fbuf.at[my_tile], dst_ref=fbuf.at[my_tile],
            send_sem=f_send.at[k], recv_sem=f_recv.at[my_tile],
            device_id={"dom": other, "rep": rep}, device_id_type=MESH,
        )

    @pl.when(is_owner)
    def _():
        total = part[rep, pl.ds(pl.multiple_of(my_tile * tile, tile), tile), :].astype(jnp.float32)
        for slot in range(1, devices):
            pltpu.make_async_copy(rbuf.at[slot], rbuf.at[slot], r_recv.at[slot]).wait()
            total = total + rbuf[slot].astype(jnp.float32)
        fbuf[my_tile] = total
        for k in range(1, dom_size):
            final_copy(k).start()

    for t in range(tiles):

        @pl.when(jnp.logical_not(jnp.logical_and(is_owner, my_tile == t)))
        def _():
            pltpu.make_async_copy(fbuf.at[t], fbuf.at[t], f_recv.at[t]).wait()

    out_ref[...] = fbuf[...]

    @pl.when(is_owner)
    def _():
        for k in range(1, dom_size):
            final_copy(k).wait_send()

    for t in range(tiles):
        for j in range(rep_size):
            target, copy = partial_copy(t, j)

            @pl.when(target != me)
            def _():
                copy.wait_send()

    for copy in sends:
        copy.wait_send()


def per_device(
    date_key, item_key, store_key, measures, block_count, item_price, store_region, date_flag
):
    dom_size = lax.axis_size("dom")
    rep_size = lax.axis_size("rep")
    devices = dom_size * rep_size
    regions = REG_DEV * dom_size
    weeks = date_flag.shape[0] // week_length
    slots = date_key.shape[0]
    half = slots // rep_size
    item_rows = item_price.shape[0] // LANES
    chunk = 16
    tile = 16
    tiles = AGGS * regions // tile
    outer = dom_size // 4
    left_bytes = rep_size * AGGS * regions * half * LANES * 2
    prebuilt = half // chunk if left_bytes <= 24 * 1024 * 1024 else 1
    bf16, f32, i32 = jnp.bfloat16, jnp.float32, jnp.int32
    dma = pltpu.SemaphoreType.DMA
    vmem = pl.BlockSpec(memory_space=pltpu.VMEM)
    hbm = pl.BlockSpec(memory_space=pl.ANY)
    facts = (half, LANES)
    out = pl.pallas_call(
        functools.partial(kernel, dom_size, rep_size, regions, item_rows, slots, chunk),
        out_shape=jax.ShapeDtypeStruct((tiles, tile, weeks // rep_size), f32),
        in_specs=[pl.BlockSpec(memory_space=pltpu.SMEM), hbm, hbm, hbm, hbm, hbm, hbm, hbm],
        out_specs=vmem,
        scratch_shapes=[
            pltpu.VMEM(facts, i32), pltpu.VMEM(facts, i32), pltpu.VMEM(facts, i32),
            pltpu.VMEM((half * 4, LANES), f32),
            pltpu.VMEM((item_rows, LANES), f32),
            pltpu.VMEM((store_region.shape[0] // LANES, LANES), i32),
            pltpu.VMEM((date_flag.shape[0] // LANES, LANES), i32),
            pltpu.VMEM((devices, round_up(item_rows, 16), LANES), bf16),
            pltpu.VMEM((2, 16, LANES), i32),
            pltpu.VMEM(facts, f32),
            pltpu.VMEM(facts, f32), pltpu.VMEM(facts, f32), pltpu.VMEM(facts, f32), pltpu.VMEM(facts, f32),
            pltpu.VMEM(facts, i32), pltpu.VMEM(facts, i32), pltpu.VMEM(facts, i32),
            pltpu.VMEM(facts, i32),
            pltpu.VMEM((prebuilt, rep_size * AGGS * regions, chunk * LANES), bf16),
            pltpu.VMEM((rep_size * AGGS * regions, weeks // rep_size), f32),
            pltpu.VMEM((rep_size, AGGS * regions, weeks // rep_size), bf16),
            pltpu.VMEM((devices, tile, weeks // rep_size), bf16),
            pltpu.VMEM((tiles, tile, weeks // rep_size), f32),
            dma((7,)),
            dma((outer - 1,)), dma((outer - 1,)),
            dma((outer,)), dma((outer,)), dma((outer,)), dma((outer,)), dma((outer,)), dma((outer,)),
            dma((4, outer)), dma((4, outer)),
            dma((tiles, rep_size)), dma((devices,)),
            dma((dom_size,)), dma((tiles,)),
        ],
        compiler_params=pltpu.CompilerParams(
            collective_id=0, has_side_effects=True, vmem_limit_bytes=60 * 1024 * 1024
        ),
        cost_estimate=pl.CostEstimate(
            flops=2 * AGGS * regions * weeks * half * LANES, bytes_accessed=half * LANES * 28, transcendentals=0
        ),
    )(
        block_count, date_key, item_key, store_key, measures.reshape(slots * 4, LANES),
        item_price.reshape(item_rows, LANES), store_region.reshape(-1, LANES), date_flag.reshape(-1, LANES),
    )
    return out.reshape(AGGS, regions, weeks // rep_size)


def solution(mesh):
    placed = (
        P("dom", None),
        P("dom", None),
        P("dom", None),
        P("dom", None, None),
        P("dom"),
        P(("dom", "rep")),
        P(),
        P(),
    )
    return jax.shard_map(
        per_device, mesh=mesh, in_specs=placed, out_specs=P(None, None, "rep"), check_vma=False
    )
```

```python
import functools

import jax
import jax.numpy as jnp
import numpy as np
from jax import lax
from jax.experimental import pallas as pl
from jax.experimental.pallas import tpu as pltpu
from jax.sharding import PartitionSpec as P

MESH = pl.DeviceIdType.MESH
AGGS = 3
REG_DEV = 2
LANES = 128
low_price = 0.2
high_price = 0.8
week_length = 7


def round_up(value, step):
    return (value + step - 1) // step * step


def divider(divisor, limit):
    n = np.arange(limit, dtype=np.int64)
    for shift in range(8, 24):
        multiplier = -(-(1 << shift) // divisor)
        if (limit * multiplier) < (1 << 31) and np.array_equal((n * multiplier) >> shift, n // divisor):
            return multiplier, shift
    raise ValueError("no divider")


def lookup(row, lane):
    return jnp.take_along_axis(jnp.broadcast_to(row, lane.shape), lane, axis=1)


def kernel(
    dom_size, rep_size, regions, item_rows, slots, chunk,
    count_ref, date_hbm, item_hbm, store_hbm, meas_hbm, price_hbm, region_hbm, flag_hbm,
    out_ref,
    date_v, item_v, store_v, meas_v, price_ref, region_ref, flag_ref,
    flags, words, reg_f, hit_f, week_f, prof_f, rev_f, qty_f, lane_i, row_i, bit_i, week_hot,
    acc, part, rbuf, fbuf,
    in_sem, z_send, z_recv, p_send, p_recv, q_send, q_recv, d_send, d_recv, c_send, c_recv,
    r_send, r_recv, f_send, f_recv,
):
    dom = lax.axis_index("dom")
    rep = lax.axis_index("rep")
    devices = dom_size * rep_size
    me = dom * rep_size + rep
    half = slots // rep_size
    outer_size = dom_size // 4
    outer = dom // 4
    mid = (dom // 2) % 2
    core = dom % 2

    base = pl.multiple_of(rep * half, 8)
    price_load = pltpu.make_async_copy(price_hbm, price_ref, in_sem.at[4])
    price_load.start()
    loads = [
        pltpu.make_async_copy(date_hbm.at[pl.ds(base, half)], date_v, in_sem.at[0]),
        pltpu.make_async_copy(item_hbm.at[pl.ds(base, half)], item_v, in_sem.at[1]),
        pltpu.make_async_copy(store_hbm.at[pl.ds(base, half)], store_v, in_sem.at[2]),
        pltpu.make_async_copy(meas_hbm.at[pl.ds(base * 4, half * 4)], meas_v, in_sem.at[3]),
        pltpu.make_async_copy(region_hbm, region_ref, in_sem.at[5]),
        pltpu.make_async_copy(flag_hbm, flag_ref, in_sem.at[6]),
    ]
    for load in loads:
        load.start()

    barrier = pltpu.get_barrier_semaphore()
    for k in range(1, devices):
        other = (me + k) % devices
        pl.semaphore_signal(
            barrier, inc=1, device_id={"dom": other // rep_size, "rep": other % rep_size}, device_id_type=MESH
        )

    padded = flags.shape[1]
    price_load.wait()
    price = price_ref[...]
    power = jnp.left_shift(jnp.ones(price.shape, jnp.int32), me % 16).astype(jnp.float32)
    mark = jnp.where((price >= low_price) & (price <= high_price), power, 0.0)
    if padded > item_rows:
        mark = jnp.concatenate([mark, jnp.zeros((padded - item_rows, LANES), jnp.float32)], axis=0)
    flags[me] = mark.astype(jnp.bfloat16)
    pl.semaphore_wait(barrier, devices - 1)

    def index_of(o, m, c, r):
        return ((o * 2 + m) * 2 + c) * rep_size + r

    sends = []

    def send(block, to_dom, to_rep, s_sem, r_sem):
        copy = pltpu.make_async_remote_copy(
            src_ref=flags.at[block], dst_ref=flags.at[block], send_sem=s_sem, recv_sem=r_sem,
            device_id={"dom": to_dom, "rep": to_rep}, device_id_type=MESH,
        )
        copy.start()
        sends.append(copy)
        return copy

    dom_mid = dom + 2 - 4 * mid
    rep_other = (rep + 1) % rep_size
    dom_core = dom + 1 - 2 * core
    first_dom, first_rep = dom + (1 - core) * (2 - 4 * mid), rep + core * (rep_other - rep)
    second_dom, second_rep = dom + core * (2 - 4 * mid), rep + (1 - core) * (rep_other - rep)
    first_mid = mid + (1 - core) * (1 - 2 * mid)

    zc, pc, qc, dc, cc = {}, {}, {}, {}, {}

    def column(k):
        o = (outer + outer_size - k) % outer_size
        block = index_of(o, mid, core, rep)
        pc[k] = send(block, first_dom, first_rep, p_send.at[k], p_recv.at[k])
        qc[k] = send(block, second_dom, second_rep, q_send.at[k], q_recv.at[k])
        cc[0, k] = send(block, dom_core, rep, c_send.at[0, k], c_recv.at[0, k])

    def got_p(k):
        pc[k].wait_recv()
        o = (outer + outer_size - k) % outer_size
        block = index_of(o, first_mid, core, first_rep)
        dc[k] = send(block, second_dom, second_rep, d_send.at[k], d_recv.at[k])
        cc[1, k] = send(block, dom_core, rep, c_send.at[1, k], c_recv.at[1, k])

    def got_q(k):
        qc[k].wait_recv()
        o = (outer + outer_size - k) % outer_size
        second_mid = mid + core * (1 - 2 * mid)
        cc[2, k] = send(index_of(o, second_mid, core, second_rep), dom_core, rep, c_send.at[2, k], c_recv.at[2, k])

    def got_d(k):
        dc[k].wait_recv()
        o = (outer + outer_size - k) % outer_size
        cc[3, k] = send(index_of(o, 1 - mid, core, rep_other), dom_core, rep, c_send.at[3, k], c_recv.at[3, k])

    for k in range(1, outer_size):
        o = (outer + k) % outer_size
        zc[k] = send(me, o * 4 + dom % 4, rep, z_send.at[k - 1], z_recv.at[k - 1])
    column(0)

    for load in loads:
        load.wait()
    date_word = flag_ref[0:1, :]
    for j in range(1, flag_ref.shape[0]):
        date_word = date_word | (flag_ref[j : j + 1, :] << j)
    week_mul, week_shift = divider(week_length, flag_ref.shape[0] * LANES)
    dev_mul, dev_shift = divider(item_rows, item_rows * devices)
    count = count_ref[0]
    cols = week_hot.shape[1]
    mid_group = regions * rep_size // 2

    def prepare(g, carry):
        start = pl.multiple_of(g * 8, 8)
        rows = pl.ds(start, 8)
        date = date_v[rows, :]
        day = (lookup(date_word, date & (LANES - 1)) >> (date >> 7)) & 1
        store = store_v[rows, :]
        region = lookup(region_ref[0:1, :], store & (LANES - 1))
        for j in range(1, region_ref.shape[0]):
            region = jnp.where((store >> 7) == j, lookup(region_ref[j : j + 1, :], store & (LANES - 1)), region)
        slot = base + start + lax.broadcasted_iota(jnp.int32, (8, LANES), 0)
        ok = (day == 1) & (slot < count)
        week = (date * week_mul) >> week_shift
        part_of = jnp.zeros(week.shape, jnp.int32)
        for j in range(1, rep_size):
            part_of = jnp.where(week >= j * cols, j, part_of)
        reg_f[rows, :] = jnp.where(ok, part_of * regions + region - mid_group, mid_group).astype(jnp.float32)
        week_f[rows, :] = (week - part_of * cols).astype(jnp.float32)
        quantity = meas_v[pl.ds(start * 4, 8, stride=4), :]
        selling = meas_v[pl.ds(start * 4 + 1, 8, stride=4), :]
        wholesale = meas_v[pl.ds(start * 4 + 2, 8, stride=4), :]
        coupon = meas_v[pl.ds(start * 4 + 3, 8, stride=4), :]
        prof_f[rows, :] = quantity * (selling - wholesale) - coupon
        rev_f[rows, :] = quantity * selling - coupon
        qty_f[rows, :] = quantity
        item = item_v[rows, :]
        page = item >> 7
        holder = (page * dev_mul) >> dev_shift
        lane_i[rows, :] = item & (LANES - 1)
        row_i[rows, :] = (holder >> 5) * item_rows + page - holder * item_rows
        bit_i[rows, :] = holder & 31
        return carry

    lax.fori_loop(0, half // 8, prepare, 0)

    column_iota = lax.broadcasted_iota(jnp.int32, (LANES, cols), 1).astype(jnp.float32)

    def build_weeks(n):
        turned = jnp.transpose(week_f[n * chunk : (n + 1) * chunk, :])
        for i in range(chunk):
            hot = jnp.where(turned[:, i : i + 1] == column_iota, 1.0, 0.0).astype(jnp.bfloat16)
            week_hot[(n * chunk + i) * LANES : (n * chunk + i + 1) * LANES, :] = hot

    chunks = half // chunk
    to_build = list(range(chunks))

    def idle():
        if to_build:
            build_weeks(to_build.pop(0))

    for k in range(outer_size):
        got_p(k)
        idle()
        if k + 1 < outer_size:
            zc[k + 1].wait_recv()
            column(k + 1)
            idle()
        got_q(k)
        idle()
        if k >= 1:
            got_d(k - 1)
    got_d(outer_size - 1)
    while to_build:
        idle()
    for k in range(outer_size):
        for j in range(4):
            cc[j, k].wait_recv()

    for g in range((devices + 31) // 32):
        word = None
        for h in range(2):
            total = None
            for b in range(16):
                device = g * 32 + h * 16 + b
                if device < devices:
                    piece = flags[device].astype(jnp.float32)
                    total = piece if total is None else total + piece
            if total is not None:
                bits = total.astype(jnp.int32)
                word = bits if h == 0 else word | (bits << 16)
        words[g * item_rows : (g + 1) * item_rows, :] = word[:item_rows]

    acc[...] = jnp.zeros(acc.shape, jnp.float32)
    word_rows = words.shape[0]
    groups = regions * rep_size
    iota = lax.broadcasted_iota(jnp.int32, (16, LANES), 0).astype(jnp.float32)
    group_iota = [(iota + (16.0 * j - mid_group)).astype(jnp.bfloat16) for j in range(groups // 16)]
    per_part = regions // 16
    zero = jnp.zeros((16, LANES), jnp.bfloat16)

    def hits(n):
        first = pl.multiple_of(n * chunk, 8)
        found_all = []
        for g in range(chunk // 8):
            rows = pl.ds(first + 8 * g, 8)
            lane, row = lane_i[rows, :], row_i[rows, :]
            found = lookup(words[0:1, :], lane)
            for w in range(1, word_rows):
                found = jnp.where(row == w, lookup(words[w : w + 1, :], lane), found)
            hit = (found >> bit_i[rows, :]) & 1
            found_all.append(jnp.where(hit == 1, reg_f[rows, :], float(mid_group)))
        return found_all

    def put(slot, found_all):
        for g in range(chunk // 8):
            hit_f[slot, 8 * g : 8 * g + 8, :] = found_all[g]

    put(0, hits(0))

    def add_chunk(n, carry):
        first = pl.multiple_of(n * chunk, 8)
        ahead = hits(jnp.minimum(n + 1, chunks - 1))
        lefts = []
        for i in range(chunk):

            def spread(row):
                return jnp.broadcast_to(row, (16, LANES)).astype(jnp.bfloat16)

            group = spread(hit_f[n % 2, i : i + 1, :])
            line = pl.ds(first + i, 1)
            values = [spread(prof_f[line, :]), spread(rev_f[line, :]), spread(qty_f[line, :])]
            masks = [one_iota == group for one_iota in group_iota]
            lefts.append(
                jnp.concatenate(
                    [
                        jnp.where(m, v, zero)
                        for j in range(rep_size)
                        for v in values
                        for m in masks[j * per_part : (j + 1) * per_part]
                    ],
                    axis=0,
                )
            )
        left = jnp.concatenate(lefts, axis=1)
        right = week_hot[pl.ds(pl.multiple_of(first * LANES, LANES), chunk * LANES), :]
        acc[...] += jnp.dot(left, right, preferred_element_type=jnp.float32)
        put((n + 1) % 2, ahead)
        return carry

    lax.fori_loop(0, chunks, add_chunk, 0)

    tile = fbuf.shape[1]
    tiles = fbuf.shape[0]
    out_rows = AGGS * regions
    for j in range(rep_size):
        part[j] = acc[j * out_rows : (j + 1) * out_rows, :].astype(jnp.bfloat16)
    my_tile = (dom * tiles + dom_size - 1) // dom_size
    is_owner = jnp.logical_and(my_tile < tiles, (my_tile * dom_size) // tiles == dom)

    def partial_copy(t, j):
        owner = t * dom_size // tiles
        target = owner * rep_size + j
        slot = (me + devices - target) % devices
        return target, pltpu.make_async_remote_copy(
            src_ref=part.at[j, pl.ds(t * tile, tile)], dst_ref=rbuf.at[slot],
            send_sem=r_send.at[t, j], recv_sem=r_recv.at[slot],
            device_id={"dom": owner, "rep": j}, device_id_type=MESH,
        )

    for t in range(tiles):
        for j in range(rep_size):
            target, copy = partial_copy(t, j)

            @pl.when(target != me)
            def _():
                copy.start()

    def final_copy(k):
        other = (dom + k) % dom_size
        return pltpu.make_async_remote_copy(
            src_ref=fbuf.at[my_tile], dst_ref=fbuf.at[my_tile],
            send_sem=f_send.at[k], recv_sem=f_recv.at[my_tile],
            device_id={"dom": other, "rep": rep}, device_id_type=MESH,
        )

    @pl.when(is_owner)
    def _():
        total = part[rep, pl.ds(pl.multiple_of(my_tile * tile, tile), tile), :].astype(jnp.float32)
        for slot in range(1, devices):
            pltpu.make_async_copy(rbuf.at[slot], rbuf.at[slot], r_recv.at[slot]).wait()
            total = total + rbuf[slot].astype(jnp.float32)
        fbuf[my_tile] = total
        for k in range(1, dom_size):
            final_copy(k).start()

    for t in range(tiles):

        @pl.when(jnp.logical_not(jnp.logical_and(is_owner, my_tile == t)))
        def _():
            pltpu.make_async_copy(fbuf.at[t], fbuf.at[t], f_recv.at[t]).wait()

    out_ref[...] = fbuf[...]

    @pl.when(is_owner)
    def _():
        for k in range(1, dom_size):
            final_copy(k).wait_send()

    for t in range(tiles):
        for j in range(rep_size):
            target, copy = partial_copy(t, j)

            @pl.when(target != me)
            def _():
                copy.wait_send()

    for copy in sends:
        copy.wait_send()


def per_device(
    date_key, item_key, store_key, measures, block_count, item_price, store_region, date_flag
):
    dom_size = lax.axis_size("dom")
    rep_size = lax.axis_size("rep")
    devices = dom_size * rep_size
    regions = REG_DEV * dom_size
    weeks = date_flag.shape[0] // week_length
    slots = date_key.shape[0]
    half = slots // rep_size
    item_rows = item_price.shape[0] // LANES
    chunk = 16
    tile = 16
    tiles = AGGS * regions // tile
    outer = dom_size // 4
    bf16, f32, i32 = jnp.bfloat16, jnp.float32, jnp.int32
    dma = pltpu.SemaphoreType.DMA
    vmem = pl.BlockSpec(memory_space=pltpu.VMEM)
    hbm = pl.BlockSpec(memory_space=pltpu.HBM)
    facts = (half, LANES)
    out = pl.pallas_call(
        functools.partial(kernel, dom_size, rep_size, regions, item_rows, slots, chunk),
        out_shape=jax.ShapeDtypeStruct((tiles, tile, weeks // rep_size), f32),
        in_specs=[pl.BlockSpec(memory_space=pltpu.SMEM), hbm, hbm, hbm, hbm, hbm, hbm, hbm],
        out_specs=vmem,
        scratch_shapes=[
            pltpu.VMEM(facts, i32), pltpu.VMEM(facts, i32), pltpu.VMEM(facts, i32),
            pltpu.VMEM((half * 4, LANES), f32),
            pltpu.VMEM((item_rows, LANES), f32),
            pltpu.VMEM((store_region.shape[0] // LANES, LANES), i32),
            pltpu.VMEM((date_flag.shape[0] // LANES, LANES), i32),
            pltpu.VMEM((devices, round_up(item_rows, 16), LANES), bf16),
            pltpu.VMEM(((devices + 31) // 32 * item_rows, LANES), i32),
            pltpu.VMEM(facts, f32), pltpu.VMEM((2, chunk, LANES), f32),
            pltpu.VMEM(facts, f32), pltpu.VMEM(facts, f32), pltpu.VMEM(facts, f32), pltpu.VMEM(facts, f32),
            pltpu.VMEM(facts, i32), pltpu.VMEM(facts, i32), pltpu.VMEM(facts, i32),
            pltpu.VMEM((half * LANES, weeks // rep_size), bf16),
            pltpu.VMEM((rep_size * AGGS * regions, weeks // rep_size), f32),
            pltpu.VMEM((rep_size, AGGS * regions, weeks // rep_size), bf16),
            pltpu.VMEM((devices, tile, weeks // rep_size), bf16),
            pltpu.VMEM((tiles, tile, weeks // rep_size), f32),
            dma((7,)),
            dma((outer - 1,)), dma((outer - 1,)),
            dma((outer,)), dma((outer,)), dma((outer,)), dma((outer,)), dma((outer,)), dma((outer,)),
            dma((4, outer)), dma((4, outer)),
            dma((tiles, rep_size)), dma((devices,)),
            dma((dom_size,)), dma((tiles,)),
        ],
        compiler_params=pltpu.CompilerParams(
            collective_id=0, has_side_effects=True, vmem_limit_bytes=40 * 1024 * 1024
        ),
        cost_estimate=pl.CostEstimate(
            flops=2 * AGGS * regions * weeks * half * LANES, bytes_accessed=half * LANES * 28, transcendentals=0
        ),
    )(
        block_count, date_key, item_key, store_key, measures.reshape(slots * 4, LANES),
        item_price.reshape(item_rows, LANES), store_region.reshape(-1, LANES), date_flag.reshape(-1, LANES),
    )
    return out.reshape(AGGS, regions, weeks // rep_size)


def solution(mesh):
    placed = (
        P("dom", None),
        P("dom", None),
        P("dom", None),
        P("dom", None, None),
        P("dom"),
        P(("dom", "rep")),
        P(),
        P(),
    )
    return jax.shard_map(
        per_device, mesh=mesh, in_specs=placed, out_specs=P(None, None, "rep"), check_vma=False
    )
```
